32 devices in a mesh: kv: 2 (over y), blk: 16 (over z, x, core).
Axes of the slice: x: 2, y: 2, z: 4, core: 2. Of those that a mesh axis runs over, the one named last changes fastest.
Arguments:
- suffix_query: bfloat16 [3072, 4096], P('blk', 'kv'), may hold values from -6 to 6
- suffix_key_value: bfloat16 [2, 3072, 2048], P(None, 'blk', 'kv'), may hold values from -6 to 6
- suffix_resid: bfloat16 [3072, 4608], P('blk', 'kv'), may hold values from -6 to 6
- decode_query_rows: bfloat16 [32, 4096], P('blk', 'kv'), may hold values from -6 to 6
- decode_key_value: bfloat16 [2, 32, 2048], P(None, 'blk', 'kv'), may hold values from -6 to 6
- decode_resid: bfloat16 [32, 4608], P('blk', 'kv'), may hold values from -6 to 6
- out_weight: bfloat16 [4096, 4608], P('kv'), may hold values from -1.125 to 1.125
- post_gain: float32 [4608], P('kv'), may hold values from 0.1 to 1.9
- prefix_page_store: bfloat16 [2, 96, 128, 2048], P(None, 'blk', None, 'kv'), may hold values from -6 to 6
- prefix_table: int32 [96], replicated, may hold values from 0 to 95, each once
- decode_page_store: bfloat16 [2, 256, 128, 2048], P(None, 'blk', None, 'kv'), may hold values from -6 to 6
- page_table: int32 [256], replicated, may hold values from 0 to 255, each once
- suffix_lengths: int32 [16], replicated, may hold values from 1 to 768, 3072 in all
- suffix_prefix: int32 [16], replicated, may hold values from 0 to 3
- decode_ages: int32 [32], replicated, may hold values from 1 to 1023, as said below
Outputs:
- suffix_hidden: bfloat16 [3072, 4608], P('blk', 'kv')
- decode_hidden: bfloat16 [32, 4608], P('blk', 'kv')
- new_cache: bfloat16 [2, 256, 128, 2048], P(None, 'blk', None, 'kv')
The draws below stay inside these ranges and needn't reach their ends.
Inputs may be any that keep to these rules, and one draw needn't show every extreme that they name: `page_table`: every page of the decode pool is named once. `prefix_table`: every page of the prefix pool is named once. `suffix_lengths`: the lengths sum to 3072; one is exactly 768. `decode_ages`: some slot has age 1024 - 1.
All inputs are finite; a program needn't handle non-finite values.
Results may differ from the reference program's by a relative error of at most 0.024.
Values may be sent and summed in bfloat16 or wider, within the bound.
A program may use at most 256 MiB of HBM per device.

```python
import math
import jax
import jax.numpy as jnp
import numpy as np
from jax import lax

D = 4608
QUERY_HEADS = 32
KEY_VALUE_HEADS = 16
HEAD_SIZE = 128
PAGE_TOKENS = 128
PREFIX_COUNT = 4
NSUF = 16
PREFIX_LENGTH = 3072
SUF_DEV = 192
SLOT_CAPACITY = 1024
SUFFIX_TOKENS = 3072
DECODE_SLOTS = 32
DECODE_PAGES = 256
PREFIX_PAGES = 96


def draw_out_weight(key, part):
    fan_in = QUERY_HEADS * HEAD_SIZE
    base = jnp.clip(jax.random.normal(key, (QUERY_HEADS * HEAD_SIZE, D), jnp.float32), -6.0, 6.0)
    column = jnp.arange(D, dtype=jnp.float32) / D
    rough = jax.random.uniform(jax.random.fold_in(key, 11), (D,), jnp.float32)
    spread = jnp.exp(1.2 * column + 1.2 * rough)
    return (base * spread[None, :] * (0.4 / fan_in ** 0.5)).astype(jnp.bfloat16)


def draw_decode_ages(key, part):
    ages = jax.random.randint(key, (DECODE_SLOTS,), 1, SLOT_CAPACITY, dtype=jnp.int32)
    target = jax.random.randint(jax.random.fold_in(key, 3), (), 0, DECODE_SLOTS, dtype=jnp.int32)
    return ages.at[target].set(SLOT_CAPACITY - 1)


def set_ends(values, own_key, smallest, top_value):
    longest = values.shape.index(max(values.shape))
    spots = []
    for shift in (0, 1):
        where = [jax.random.randint(jax.random.fold_in(own_key, axis), (), 0, length) for axis, length in enumerate(values.shape)]
        where[longest] = (where[longest] + shift) % values.shape[longest]
        spots.append(tuple(where))
    return values.at[spots[0]].set(smallest).at[spots[1]].set(top_value)


def block_scale(key, extent, shards, low, top_value):
    def one(position, blocks):
        heights = jax.random.uniform(jax.random.fold_in(jax.random.fold_in(key, 6), position), (blocks,), jnp.float32, low / len(shards), top_value / len(shards))
        return jnp.repeat(jnp.exp(heights), extent[position] // blocks).reshape((-1,) + (1,) * (len(extent) - position - 1))

    factor_of = one(*shards[0])
    for cut in shards[1:]:
        factor_of = factor_of * one(*cut)
    return factor_of


def rank_bounds(count, skew):
    portions = [(1 << 20) // math.isqrt(rank ** skew) + 1 for rank in range(1, count + 1)]
    width = 1 + sum(portions) // (1 << 30)
    return np.cumsum(np.array([max(1, weight // width) for weight in portions]))


def ranked_ids(own_key, shape, amount, slope):
    table = rank_bounds(amount, slope)
    ticket = jax.random.randint(jax.random.fold_in(own_key, 1), shape, 0, int(table[amount - 1]))
    grade = jnp.searchsorted(jnp.asarray(table, jnp.int32), ticket, side="right")
    return jax.random.permutation(jax.random.fold_in(own_key, 2), amount)[grade].astype(jnp.int32)


def profile(count, total, most, lean):
    portions = [(1 << 20) // math.isqrt(grade ** lean) + 1 for grade in range(2, count + 1)]
    rest, holding = total - most - (count - 1), [1] * (count - 1)
    while rest > 0:
        candidates = [i for i in range(count - 1) if holding[i] < most]
        mass, budget = sum([portions[i] for i in candidates]), rest
        for i in candidates:
            more = min(most - holding[i], max(1, budget * portions[i] // mass), rest)
            holding[i] = holding[i] + more
            rest = rest - more
    return np.array([most] + holding)


def ragged(rng, amount, total, bound, slope):
    if amount == 2:
        one = jax.random.randint(rng, (), max(1, total - bound), min(bound, total - 1) + 1)
        return jnp.stack([one, total - one])
    lengths = jnp.asarray(profile(amount, total, bound, slope), jnp.int32)
    pairs = (amount - 1) // 2
    donor, taker = lengths[1:1 + 2 * pairs:2], lengths[2:2 + 2 * pairs:2]
    room = jnp.minimum(donor - 1, bound - taker)
    moved = jax.random.randint(jax.random.fold_in(rng, 1), (pairs,), 0, 1 << 20) % (room + 1)
    lengths = lengths.at[1:1 + 2 * pairs:2].set(donor - moved).at[2:2 + 2 * pairs:2].set(taker + moved)
    return lengths[jax.random.permutation(jax.random.fold_in(rng, 2), amount)]


def normal_values(stream_key, dims, width, limit, pieces=(), kind=jnp.bfloat16):
    values = jax.random.normal(stream_key, dims, jnp.float32) * width
    if len(pieces) > 0:
        values = block_scale(stream_key, dims, pieces, -0.22, 0.18) * values
    return jnp.clip(values, min=-limit, max=limit).astype(kind)


def setup_inputs(seed: int = 0) -> dict:
    key_list = jax.random.split(jax.random.key(seed), 16)
    return {
        "suffix_query": normal_values(key_list[0], (SUFFIX_TOKENS, QUERY_HEADS * HEAD_SIZE), 1.0, 6.0, ((0, 16), (1, 2))),
        "suffix_key_value": normal_values(key_list[1], (2, SUFFIX_TOKENS, KEY_VALUE_HEADS * HEAD_SIZE), 1.0, 6.0, ((1, 16), (2, 2))),
        "suffix_resid": normal_values(key_list[2], (SUFFIX_TOKENS, D), 1.0, 6.0, ((0, 16), (1, 2))),
        "decode_query_rows": normal_values(key_list[3], (DECODE_SLOTS, QUERY_HEADS * HEAD_SIZE), 1.0, 6.0, ((0, 16), (1, 2))),
        "decode_key_value": normal_values(key_list[4], (2, DECODE_SLOTS, KEY_VALUE_HEADS * HEAD_SIZE), 1.0, 6.0, ((1, 16), (2, 2))),
        "decode_resid": normal_values(key_list[5], (DECODE_SLOTS, D), 1.0, 6.0, ((0, 16), (1, 2))),
        "out_weight": draw_out_weight(jax.random.fold_in(key_list[15], 71), 0),
        "post_gain": jnp.clip(1.0 + 0.18 * jax.random.normal(key_list[7], (D,), jnp.float32), 0.1, 1.9),
        "prefix_page_store": normal_values(key_list[8], (2, PREFIX_PAGES, PAGE_TOKENS, KEY_VALUE_HEADS * HEAD_SIZE), 1.0, 6.0, ((1, 16), (3, 2))),
        "prefix_table": jax.random.permutation(key_list[9], PREFIX_PAGES).astype(jnp.int32),
        "decode_page_store": normal_values(key_list[10], (2, DECODE_PAGES, PAGE_TOKENS, KEY_VALUE_HEADS * HEAD_SIZE), 1.0, 6.0, ((1, 16), (3, 2))),
        "page_table": jax.random.permutation(key_list[11], DECODE_PAGES).astype(jnp.int32),
        "suffix_lengths": ragged(key_list[12], NSUF, SUFFIX_TOKENS, 4 * SUF_DEV, 1).astype(jnp.int32),
        "suffix_prefix": set_ends(ranked_ids(key_list[13], (NSUF,), PREFIX_COUNT, 2), jax.random.fold_in(key_list[13], 3), 0, PREFIX_COUNT - 1).astype(jnp.int32),
        "decode_ages": draw_decode_ages(jax.random.fold_in(key_list[15], 71), 0),
    }


soft_cap = 50.0
norm_eps = 1e-06

def rounded(weights):
    half = weights.astype(jnp.bfloat16)
    half = lax.optimization_barrier(half)
    return half.astype(jnp.float32)

def attend(query_rows, key_rows, value_rows, visible, q_scale):
    logits = jnp.einsum('qhgd,khd->qhgk', query_rows.astype(jnp.float32), key_rows.astype(jnp.float32)) * q_scale
    capped = soft_cap * jnp.tanh(logits / soft_cap)
    weights = jnp.where(visible[:, None, None, :], jnp.exp(capped), 0.0)
    denominator = lax.optimization_barrier(jnp.sum(weights, axis=3))
    numerator = jnp.einsum('qhgk,khd->qhgd', rounded(weights), value_rows.astype(jnp.float32))
    return (numerator, denominator)

def suffix_part(suffix_query, suffix_key_value, prefix_page_store, prefix_table, suffix_lengths, suffix_prefix):
    query_group_width = QUERY_HEADS // KEY_VALUE_HEADS
    token_extent = 4 * SUF_DEV
    q_scale = (D // QUERY_HEADS) ** (-0.5)
    per_prefix = PREFIX_LENGTH // PAGE_TOKENS
    prefix_page_list = prefix_page_store[:, prefix_table.reshape(PREFIX_COUNT, per_prefix)]
    prefix_key_rows = prefix_page_list[0].reshape(PREFIX_COUNT, PREFIX_LENGTH, KEY_VALUE_HEADS, HEAD_SIZE)
    prefix_value_rows = prefix_page_list[1].reshape(PREFIX_COUNT, PREFIX_LENGTH, KEY_VALUE_HEADS, HEAD_SIZE)
    padded_query = jnp.concatenate([suffix_query, jnp.zeros((token_extent, QUERY_HEADS * HEAD_SIZE), suffix_query.dtype)], axis=0)
    padded_query = padded_query.reshape(SUFFIX_TOKENS + token_extent, KEY_VALUE_HEADS, query_group_width, HEAD_SIZE)
    padded_key_value = jnp.concatenate([suffix_key_value, jnp.zeros((2, token_extent, KEY_VALUE_HEADS * HEAD_SIZE), suffix_key_value.dtype)], axis=1)
    padded_key_value = padded_key_value.reshape(2, SUFFIX_TOKENS + token_extent, KEY_VALUE_HEADS, HEAD_SIZE)
    suffix_ends = jnp.cumsum(suffix_lengths).astype(jnp.int32)
    starts = (suffix_ends - suffix_lengths).astype(jnp.int32)
    places = jnp.arange(token_extent, dtype=jnp.int32)
    causal = places[None, :] <= places[:, None]
    everyone = jnp.ones((token_extent, PREFIX_LENGTH), dtype=bool)

    def one_suffix(result, index):
        first = starts[index]
        length_now = suffix_lengths[index]
        owner = suffix_prefix[index]
        q_window = lax.dynamic_slice_in_dim(padded_query, first, token_extent, 0)
        k_window = lax.dynamic_slice_in_dim(padded_key_value[0], first, token_extent, 0)
        v_window = lax.dynamic_slice_in_dim(padded_key_value[1], first, token_extent, 0)
        pre_keys = lax.dynamic_index_in_dim(prefix_key_rows, owner, 0, keepdims=False)
        pre_values = lax.dynamic_index_in_dim(prefix_value_rows, owner, 0, keepdims=False)
        numer_one, denom_one = attend(q_window, pre_keys, pre_values, everyone, q_scale)
        visible = causal & (places[None, :] < length_now)
        numer_two, denom_two = attend(q_window, k_window, v_window, visible, q_scale)
        output = ((numer_one + numer_two) / (denom_one + denom_two)[..., None]).astype(jnp.bfloat16)
        result = lax.dynamic_update_slice_in_dim(result, output.reshape(token_extent, QUERY_HEADS * HEAD_SIZE), first, 0)
        return (result, None)
    result = jnp.zeros((SUFFIX_TOKENS + token_extent, QUERY_HEADS * HEAD_SIZE), jnp.bfloat16)
    result, _ = lax.scan(one_suffix, result, jnp.arange(NSUF, dtype=jnp.int32))
    return result[:SUFFIX_TOKENS]

def decode_part(decode_query_rows, decode_key_value, decode_page_store, page_table, decode_ages):
    query_group_width = QUERY_HEADS // KEY_VALUE_HEADS
    q_scale = (D // QUERY_HEADS) ** (-0.5)
    slot_pages = SLOT_CAPACITY // PAGE_TOKENS
    table = page_table.reshape(DECODE_SLOTS, slot_pages)
    slot_ids = jnp.arange(DECODE_SLOTS, dtype=jnp.int32)
    target = table[slot_ids, (decode_ages // PAGE_TOKENS).astype(jnp.int32)]
    offsets = (decode_ages % PAGE_TOKENS).astype(jnp.int32)
    refreshed_cache = decode_page_store.at[:, target, offsets].set(decode_key_value)
    query_rows = decode_query_rows.reshape(DECODE_SLOTS, KEY_VALUE_HEADS, query_group_width, HEAD_SIZE)

    def one_slot(element):
        slot_query, slot_page_map, slot_age = element
        sequence_index = refreshed_cache[:, slot_page_map].reshape(2, SLOT_CAPACITY, KEY_VALUE_HEADS, HEAD_SIZE)
        visible = (jnp.arange(SLOT_CAPACITY, dtype=jnp.int32) <= slot_age)[None, :]
        numerator, denominator = attend(slot_query[None], sequence_index[0], sequence_index[1], visible, q_scale)
        return (numerator / denominator[..., None])[0].astype(jnp.bfloat16).reshape(QUERY_HEADS * HEAD_SIZE)
    output = lax.map(one_slot, (query_rows, table, decode_ages))
    return (output, refreshed_cache)

def reference(suffix_query, suffix_key_value, suffix_resid, decode_query_rows, decode_key_value, decode_resid, out_weight, post_gain, prefix_page_store, prefix_table, decode_page_store, page_table, suffix_lengths, suffix_prefix, decode_ages):
    suffix_attn = suffix_part(suffix_query, suffix_key_value, prefix_page_store, prefix_table, suffix_lengths, suffix_prefix)
    decode_attn, new_cache = decode_part(decode_query_rows, decode_key_value, decode_page_store, page_table, decode_ages)
    attention = jnp.concatenate([suffix_attn, decode_attn], axis=0)
    projected = jnp.dot(attention, out_weight, preferred_element_type=jnp.float32)
    mean_square = lax.optimization_barrier(jnp.mean(projected * projected, axis=1, keepdims=True))
    normed = projected * lax.rsqrt(mean_square + norm_eps) * post_gain.astype(jnp.float32)[None, :]
    residual = jnp.concatenate([suffix_resid, decode_resid], axis=0).astype(jnp.float32)
    hidden = (residual + normed).astype(jnp.bfloat16)
    return (hidden[:SUFFIX_TOKENS], hidden[SUFFIX_TOKENS:], new_cache)
```

```python
import functools
import math

import jax
import jax.numpy as jnp
from jax import lax
from jax.experimental import pallas as pl
from jax.experimental.pallas import tpu as pltpu
from jax.sharding import PartitionSpec as P

D = 4608
QUERY_HEADS = 32
HEAD_SIZE = 128
PAGE_TOKENS = 128
PREFIX_LENGTH = 3072
SLOT_CAPACITY = 1024


soft_cap = 50.0
norm_eps = 1e-06


def token_tables(lengths, prefix_ids, token_ids):
    suffix_ends = jnp.cumsum(lengths)
    starts = suffix_ends - lengths
    inside = (
        (token_ids[:, None] >= starts[None, :]) & (token_ids[:, None] < suffix_ends[None, :])
    ).astype(jnp.int32)
    tok_start = jnp.sum(inside * starts[None, :], axis=1)
    tok_prefix = jnp.sum(inside * prefix_ids[None, :], axis=1)
    return (tok_start, tok_prefix)


def inverse_rows(table, wanted):
    hits = (table[None, :] == wanted[:, None]).astype(jnp.int32)
    places = jnp.arange(table.shape[0], dtype=jnp.int32)
    return jnp.sum(hits * places[None, :], axis=1)


TILE = 128


def attention_kernel(
    order,
    offsets,
    flags,
    low,
    high,
    group_base,
    q_ref,
    start_ref,
    prefix_ref,
    kv_ref,
    numer_ref,
    denom_ref,
    keys,
    values,
    own_keys,
    own_values,
    acc,
    wacc,
    sems,
    *,
    prefixes,
    sources,
    local_pages,
    tok_rows,
    q_scale,
):
    page_len = PAGE_TOKENS
    tile = pl.program_id(0)

    @pl.when(tile == 0)
    def _():
        def fetch_page(i, carry):
            entry = order[i]
            j = entry // local_pages
            rows = pl.ds(pl.multiple_of((entry % local_pages) * page_len, page_len), page_len)
            to = pl.ds(pl.multiple_of(i * page_len, page_len), page_len)
            pltpu.make_async_copy(kv_ref.at[j, 0, rows], keys.at[to], sems.at[0]).start()
            pltpu.make_async_copy(kv_ref.at[j, 1, rows], values.at[to], sems.at[1]).start()
            return carry

        lax.fori_loop(0, sources * local_pages, fetch_page, 0)
        for j in range(sources):
            rows = pl.ds(local_pages * page_len, tok_rows)
            to = pl.ds(j * tok_rows, tok_rows)
            pltpu.make_async_copy(kv_ref.at[j, 0, rows], own_keys.at[to], sems.at[2]).start()
            pltpu.make_async_copy(kv_ref.at[j, 1, rows], own_values.at[to], sems.at[3]).start()
        pltpu.make_async_copy(keys, keys, sems.at[0]).wait()
        pltpu.make_async_copy(values, values, sems.at[1]).wait()
        pltpu.make_async_copy(own_keys, own_keys, sems.at[2]).wait()
        pltpu.make_async_copy(own_values, own_values, sems.at[3]).wait()

    q = q_ref[...]
    half = HEAD_SIZE
    rows_q = jnp.concatenate([q[:, :half], q[:, half:]], axis=0)
    row_prefix = prefix_ref[...]
    row_prefix = jnp.concatenate([row_prefix, row_prefix], axis=0)
    row_start = start_ref[...]
    row_start = jnp.concatenate([row_start, row_start], axis=0)
    acc[...] = jnp.zeros_like(acc)
    wacc[...] = jnp.zeros_like(wacc)
    inner = q_scale / soft_cap
    outer = soft_cap * math.log2(math.e)

    def weights_of(key_rows):
        logits = lax.dot_general(
            rows_q, key_rows, (((1,), (1,)), ((), ())), preferred_element_type=jnp.float32
        )
        return jnp.exp2(jnp.tanh(logits * inner) * outer)

    def folded(w):
        out = w[:, :half]
        for k in range(1, w.shape[1] // half):
            out = out + w[:, k * half : (k + 1) * half]
        return out

    for p in range(prefixes):

        @pl.when(flags[tile * prefixes + p] != 0)
        def _():
            first = offsets[p]
            count = offsets[p + 1] - first

            def step(width):
                def run(c, carry):
                    num, den = carry
                    at = pl.ds(
                        pl.multiple_of((first + c) * page_len, page_len), width * page_len
                    )
                    w = weights_of(keys[at, :])
                    num = num + jnp.dot(
                        w.astype(jnp.bfloat16), values[at, :], preferred_element_type=jnp.float32
                    )
                    return num, den + folded(w)

                return run

            zero = jnp.zeros((2 * TILE, half), jnp.float32)
            four = step(4)
            carry = lax.fori_loop(0, count // 4, lambda c, s: four(4 * c, s), (zero, zero))
            num, den = lax.fori_loop(count // 4 * 4, count, step(1), carry)
            mine = row_prefix == p
            acc[...] += jnp.where(mine, num, 0.0)
            wacc[...] += jnp.where(mine, den, 0.0)

    row_id = tile * TILE + lax.broadcasted_iota(jnp.int32, (TILE, 1), 0)
    row_id = jnp.concatenate([row_id, row_id], axis=0)

    def own(c, carry):
        at = pl.ds(pl.multiple_of(c * TILE, TILE), TILE)
        key_id = (
            group_base[0] + c * TILE + lax.broadcasted_iota(jnp.int32, (2 * TILE, TILE), 1)
        )
        seen = (key_id >= row_start) & (key_id <= row_id)
        w = jnp.where(seen, weights_of(own_keys[at, :]), 0.0)
        acc[...] += jnp.dot(
            w.astype(jnp.bfloat16), own_values[at, :], preferred_element_type=jnp.float32
        )
        wacc[...] += w
        return carry

    lax.fori_loop(low[tile], high[tile], own, 0)
    numer_ref[...] = jnp.concatenate([acc[:TILE, :], acc[TILE:, :]], axis=1).astype(
        numer_ref.dtype
    )
    denom_ref[0] = lax.dot_general(
        jnp.ones((8, half), jnp.float32),
        wacc[...],
        (((1,), (1,)), ((), ())),
        preferred_element_type=jnp.float32,
        precision=lax.Precision.HIGHEST,
    )


def head_attention(q_all, kv_group, tok_start, tok_prefix, page_owner, base_page, base_token,
                   prefixes, local_pages, tok_rows, q_scale):
    tokens, width = q_all.shape
    sources = kv_group.shape[0]
    pages = sources * local_pages
    tiles = tokens // TILE
    owned = lax.dynamic_slice_in_dim(page_owner, base_page, pages, 0)
    place = jnp.arange(pages, dtype=jnp.int32)
    rank = owned * pages + place
    position = jnp.sum((rank[None, :] < rank[:, None]).astype(jnp.int32), axis=1)
    order = jnp.sum(
        (position[None, :] == place[:, None]).astype(jnp.int32) * place[None, :], axis=1
    )
    ids = jnp.arange(prefixes + 1, dtype=jnp.int32)
    offsets = jnp.sum((owned[None, :] < ids[:, None]).astype(jnp.int32), axis=1)
    tile_prefix = tok_prefix.reshape(tiles, TILE)
    flags = (
        jnp.any(tile_prefix[:, :, None] == ids[None, None, :prefixes], axis=1)
        .astype(jnp.int32)
        .reshape(-1)
    )
    group_tokens = sources * tok_rows
    tile_first = jnp.arange(tiles, dtype=jnp.int32) * TILE
    low = jnp.clip(tok_start.reshape(tiles, TILE)[:, 0] - base_token, 0, group_tokens) // TILE
    high = (jnp.clip(tile_first + TILE - base_token, 0, group_tokens) + TILE - 1) // TILE
    run = functools.partial(
        attention_kernel,
        prefixes=prefixes,
        sources=sources,
        local_pages=local_pages,
        tok_rows=tok_rows,
        q_scale=q_scale,
    )
    return pl.pallas_call(
        run,
        out_shape=(
            jax.ShapeDtypeStruct((tokens, width), jnp.bfloat16),
            jax.ShapeDtypeStruct((tiles, 8, 2 * TILE), jnp.float32),
        ),
        grid_spec=pltpu.PrefetchScalarGridSpec(
            num_scalar_prefetch=6,
            grid=(tiles,),
            in_specs=[
                pl.BlockSpec((TILE, width), lambda i, *_: (i, 0)),
                pl.BlockSpec((TILE, 1), lambda i, *_: (i, 0)),
                pl.BlockSpec((TILE, 1), lambda i, *_: (i, 0)),
                pl.BlockSpec(memory_space=pl.ANY),
            ],
            out_specs=[
                pl.BlockSpec((TILE, width), lambda i, *_: (i, 0)),
                pl.BlockSpec((1, 8, 2 * TILE), lambda i, *_: (i, 0, 0)),
            ],
            scratch_shapes=[
                pltpu.VMEM((pages * PAGE_TOKENS, HEAD_SIZE), jnp.bfloat16),
                pltpu.VMEM((pages * PAGE_TOKENS, HEAD_SIZE), jnp.bfloat16),
                pltpu.VMEM((group_tokens, HEAD_SIZE), jnp.bfloat16),
                pltpu.VMEM((group_tokens, HEAD_SIZE), jnp.bfloat16),
                pltpu.VMEM((2 * TILE, HEAD_SIZE), jnp.float32),
                pltpu.VMEM((2 * TILE, HEAD_SIZE), jnp.float32),
                pltpu.SemaphoreType.DMA((4,)),
            ],
        ),
        compiler_params=pltpu.CompilerParams(vmem_limit_bytes=32 * 1024 * 1024),
        name="head_attention",
    )(order, offsets, flags, low, high, base_token[None], q_all, tok_start[:, None],
      tok_prefix[:, None], kv_group)


def body(
    suffix_query,
    suffix_key_value,
    suffix_resid,
    decode_query_rows,
    decode_key_value,
    decode_resid,
    out_weight,
    post_gain,
    prefix_page_store,
    prefix_table,
    decode_page_store,
    page_table,
    suffix_lengths,
    suffix_prefix,
    decode_ages,
):
    head_dim = HEAD_SIZE
    page_len = PAGE_TOKENS
    q_scale = (D // QUERY_HEADS) ** (-0.5)
    tok_rows = suffix_query.shape[0]
    q_heads = suffix_query.shape[1] // head_dim
    kv_heads = suffix_key_value.shape[2] // head_dim
    query_group_width = q_heads // kv_heads
    my_index = lax.axis_index("blk")
    blocks = lax.axis_size("blk")
    groups = blocks // kv_heads
    group = my_index // kv_heads
    pair = query_group_width * head_dim
    all_tokens = blocks * tok_rows
    all_ids = jnp.arange(all_tokens, dtype=jnp.int32)
    tok_start, tok_prefix = token_tables(suffix_lengths, suffix_prefix, all_ids)
    pool_pages = prefix_table.shape[0]
    per_prefix = PREFIX_LENGTH // PAGE_TOKENS
    page_owner = (
        inverse_rows(prefix_table, jnp.arange(pool_pages, dtype=jnp.int32)) // per_prefix
    )
    local_pages = prefix_page_store.shape[1]
    q_send = suffix_query.reshape(tok_rows, kv_heads, pair).transpose(1, 0, 2)
    q_send = jnp.broadcast_to(q_send[None], (groups,) + q_send.shape)
    q_send = q_send.reshape(blocks, tok_rows, pair)
    q_all = lax.all_to_all(q_send, "blk", 0, 0, tiled=True).reshape(all_tokens, pair)
    kv_send = jnp.concatenate(
        [prefix_page_store.reshape(2, local_pages * page_len, -1), suffix_key_value], axis=1
    )
    kv_send = kv_send.reshape(2, -1, kv_heads, head_dim).transpose(2, 0, 1, 3)
    members = [[g * kv_heads + h for h in range(kv_heads)] for g in range(groups)]
    kv_group = lax.all_to_all(
        kv_send, "blk", 0, 0, tiled=True, axis_index_groups=members
    )
    numer, denom = head_attention(
        q_all,
        kv_group,
        tok_start,
        tok_prefix,
        page_owner,
        group * kv_heads * local_pages,
        group * kv_heads * tok_rows,
        pool_pages // per_prefix,
        local_pages,
        tok_rows,
        q_scale,
    )
    denom = denom[:, 0, :].reshape(-1, query_group_width, TILE).transpose(1, 0, 2)
    denom = denom.reshape(query_group_width, blocks, tok_rows).transpose(1, 0, 2)
    numer = lax.all_to_all(numer.reshape(blocks, tok_rows, pair), "blk", 0, 0, tiled=True)
    denom = lax.all_to_all(denom, "blk", 0, 0, tiled=True)
    numer = numer.reshape(groups, kv_heads, tok_rows, query_group_width, head_dim)
    numer = jnp.sum(numer.astype(jnp.float32), axis=0)
    denom = jnp.sum(denom.reshape(groups, kv_heads, query_group_width, tok_rows), axis=0)
    suffix_attn = numer / denom.transpose(0, 2, 1)[..., None]
    suffix_attn = suffix_attn.astype(jnp.bfloat16).transpose(1, 0, 2, 3)
    suffix_attn = suffix_attn.reshape(tok_rows, q_heads * head_dim)
    all_dq, all_dkv = (
        lax.all_gather(decode_query_rows, "blk", axis=0, tiled=True),
        lax.all_gather(decode_key_value, "blk", axis=1, tiled=True),
    )
    slot_total = all_dq.shape[0]
    slot_pages = SLOT_CAPACITY // PAGE_TOKENS
    local_cache = decode_page_store.shape[1]
    page_ids = my_index * local_cache + jnp.arange(local_cache, dtype=jnp.int32)
    position = inverse_rows(page_table, page_ids)
    slot_of = position // slot_pages
    block_of = position % slot_pages
    slot_hot = slot_of[:, None] == jnp.arange(slot_total, dtype=jnp.int32)[None, :]
    page_age = jnp.sum(slot_hot.astype(jnp.int32) * decode_ages[None, :], axis=1)
    select = slot_hot.astype(jnp.bfloat16)
    new_rows = jnp.einsum(
        "ls,tsc->tlc", select, all_dkv, preferred_element_type=jnp.float32
    ).astype(jnp.bfloat16)
    write_here = (block_of == page_age // page_len)[:, None] & (
        jnp.arange(page_len, dtype=jnp.int32)[None, :] == (page_age % page_len)[:, None]
    )
    new_cache = jnp.where(write_here[None, :, :, None], new_rows[:, :, None, :], decode_page_store)
    page_queries = jnp.dot(select, all_dq, preferred_element_type=jnp.float32).astype(jnp.bfloat16)
    page_queries = page_queries.reshape(local_cache, kv_heads, query_group_width, head_dim)
    key_cache = new_cache[0].reshape(local_cache, page_len, kv_heads, head_dim)
    value_cache = new_cache[1].reshape(local_cache, page_len, kv_heads, head_dim)
    logits = (
        jnp.einsum("lhgd,lphd->lhgp", page_queries, key_cache, preferred_element_type=jnp.float32)
        * q_scale
    )
    capped = soft_cap * jnp.tanh(logits / soft_cap)
    places = block_of[:, None] * page_len + jnp.arange(page_len, dtype=jnp.int32)[None, :]
    seen_pos = places <= page_age[:, None]
    weights = jnp.where(seen_pos[:, None, None, :], jnp.exp(capped), 0.0)
    page_denom = jnp.sum(weights, axis=3)
    page_numer = jnp.einsum(
        "lhgp,lphd->lhgd",
        weights.astype(jnp.bfloat16),
        value_cache,
        preferred_element_type=jnp.float32,
    )
    slot_float = slot_hot.astype(jnp.float32)
    slot_numer = jnp.einsum(
        "ls,lhgd->shgd", slot_float, page_numer, precision=lax.Precision.HIGHEST
    )
    slot_denom = jnp.einsum("ls,lhg->shg", slot_float, page_denom, precision=lax.Precision.HIGHEST)
    mine_numer, mine_denom = (
        lax.psum_scatter(
            slot_numer.astype(jnp.bfloat16), "blk", scatter_dimension=0, tiled=True
        ).astype(jnp.float32),
        lax.psum_scatter(
            slot_denom.astype(jnp.bfloat16), "blk", scatter_dimension=0, tiled=True
        ).astype(jnp.float32),
    )
    decode_attn = (mine_numer / mine_denom[..., None]).astype(jnp.bfloat16)
    decode_rows = decode_attn.shape[0]
    decode_attn = decode_attn.reshape(decode_rows, q_heads * head_dim)
    attention = jnp.concatenate([suffix_attn, decode_attn], axis=0)
    projected = jnp.dot(attention, out_weight, preferred_element_type=jnp.float32)
    residual = jnp.concatenate([suffix_resid, decode_resid], axis=0).astype(jnp.float32)
    mine = lax.psum_scatter(
        projected.astype(jnp.bfloat16), "kv", scatter_dimension=1, tiled=True
    ).astype(jnp.float32)
    mean_square = lax.psum(jnp.sum(mine * mine, axis=1), "kv") / D
    normed = mine * lax.rsqrt(mean_square + norm_eps)[:, None] * post_gain[None, :]
    hidden = (residual + normed).astype(jnp.bfloat16)
    return (hidden[:tok_rows], hidden[tok_rows:], new_cache)


def solution(mesh):
    placed = (
        P("blk", "kv"),
        P(None, "blk", "kv"),
        P("blk", "kv"),
        P("blk", "kv"),
        P(None, "blk", "kv"),
        P("blk", "kv"),
        P("kv", None),
        P("kv"),
        P(None, "blk", None, "kv"),
        P(),
        P(None, "blk", None, "kv"),
        P(),
        P(),
        P(),
        P(),
    )
    return jax.shard_map(
        body,
        mesh=mesh,
        in_specs=placed,
        out_specs=(P("blk", "kv"), P("blk", "kv"), P(None, "blk", None, "kv")),
        check_vma=False,
    )
```

```python
import functools
import math

import jax
import jax.numpy as jnp
from jax import lax
from jax.experimental import pallas as pl
from jax.experimental.pallas import tpu as pltpu
from jax.sharding import PartitionSpec as P

D = 4608
QUERY_HEADS = 32
HEAD_SIZE = 128
PAGE_TOKENS = 128
PREFIX_LENGTH = 3072
SLOT_CAPACITY = 1024


soft_cap = 50.0
norm_eps = 1e-06


def token_tables(lengths, prefix_ids, token_ids):
    suffix_ends = jnp.cumsum(lengths)
    starts = suffix_ends - lengths
    inside = (
        (token_ids[:, None] >= starts[None, :]) & (token_ids[:, None] < suffix_ends[None, :])
    ).astype(jnp.int32)
    tok_start = jnp.sum(inside * starts[None, :], axis=1)
    tok_prefix = jnp.sum(inside * prefix_ids[None, :], axis=1)
    return (tok_start, tok_prefix)


def inverse_rows(table, wanted):
    hits = (table[None, :] == wanted[:, None]).astype(jnp.int32)
    places = jnp.arange(table.shape[0], dtype=jnp.int32)
    return jnp.sum(hits * places[None, :], axis=1)


PARTS = 2


def attention_kernel(
    places,
    offsets,
    flags,
    low,
    high,
    group_base,
    q_ref,
    start_ref,
    prefix_ref,
    kv_ref,
    numer_ref,
    denom_ref,
    acc,
    wacc,
    *,
    part,
    prefixes,
    local_pages,
    tok_rows,
    q_scale,
):
    page_len = PAGE_TOKENS
    tile_rows = q_ref.shape[1]
    section = local_pages * page_len + tok_rows
    tile = pl.program_id(0)
    q = q_ref[0]
    half = HEAD_SIZE
    rows_q = jnp.concatenate([q[:, :half], q[:, half:]], axis=0)
    row_prefix = prefix_ref[...]
    row_prefix = jnp.concatenate([row_prefix, row_prefix], axis=0)
    row_start = start_ref[...]
    row_start = jnp.concatenate([row_start, row_start], axis=0)
    inner = q_scale / soft_cap
    outer = soft_cap * math.log2(math.e)

    def weights_of(key_rows):
        logits = lax.dot_general(
            rows_q, key_rows, (((1,), (1,)), ((), ())), preferred_element_type=jnp.float32
        )
        return jnp.exp2(jnp.tanh(logits * inner) * outer)

    def folded(w):
        out = w[:, :half]
        for k in range(1, w.shape[1] // half):
            out = out + w[:, k * half : (k + 1) * half]
        return out

    def load(row, length):
        return kv_ref[pl.ds(pl.multiple_of(row, 64), length), :]

    row_id = (tile * PARTS + part) * tile_rows + lax.broadcasted_iota(
        jnp.int32, (tile_rows, 1), 0
    )
    row_id = jnp.concatenate([row_id, row_id], axis=0)
    acc[...] = jnp.zeros_like(acc)
    wacc[...] = jnp.zeros_like(wacc)
    span = 256

    def own(c, carry):
        first = group_base[0] + c * tok_rows
        row = (2 * c + 1) * section - span
        key_id = first + (tok_rows - span) + lax.broadcasted_iota(jnp.int32, (1, span), 1)
        seen = (key_id >= jnp.maximum(row_start, first)) & (key_id <= row_id)
        w = jnp.where(seen, weights_of(load(row, span)), 0.0)
        acc[...] += jnp.dot(
            w.astype(jnp.bfloat16), load(row + section, span), preferred_element_type=jnp.float32
        )
        wacc[...] += folded(w)
        return carry

    lax.fori_loop(low[tile], high[tile], own, 0)

    for p in range(prefixes):

        @pl.when(flags[tile * prefixes + p] != 0)
        def _():
            first = offsets[p]
            count = offsets[p + 1] - first
            keep = jnp.where(row_prefix == p, 1.0, 0.0)

            def step(width, c):
                rows = [places[first + c + k] for k in range(width)]
                key_rows = jnp.concatenate([load(r, page_len) for r in rows], axis=0)
                value_rows = jnp.concatenate([load(r + section, page_len) for r in rows], axis=0)
                w = weights_of(key_rows)
                num = jnp.dot(
                    w.astype(jnp.bfloat16), value_rows, preferred_element_type=jnp.float32
                )
                acc[...] += num * keep
                wacc[...] += folded(w) * keep

            def eight(c, carry):
                step(8, 8 * c)
                return carry

            lax.fori_loop(0, count // 8, eight, 0)
            for width in (4, 2, 1):

                @pl.when(count // width % 2 == 1)
                def _():
                    step(width, count // (2 * width) * (2 * width))

    numer_ref[0] = jnp.concatenate(
        [acc[:tile_rows, :], acc[tile_rows:, :]], axis=1
    ).astype(numer_ref.dtype)
    denom_ref[0] = lax.dot_general(
        jnp.ones((8, half), jnp.float32),
        wacc[...],
        (((1,), (1,)), ((), ())),
        preferred_element_type=jnp.float32,
        precision=lax.Precision.HIGHEST,
    )


def head_attention(part, q_part, kv_group, tok_start, tok_prefix, plan, base_token,
                   prefixes, local_pages, tok_rows, q_scale):
    tiles, tile_rows, width = q_part.shape
    sources = kv_group.shape[0]
    places, offsets = plan
    tile_start = tok_start.reshape(tiles, PARTS, tile_rows)[:, part]
    tile_prefix = tok_prefix.reshape(tiles, PARTS, tile_rows)[:, part]
    ids = jnp.arange(prefixes, dtype=jnp.int32)
    flags = jnp.any(tile_prefix[:, :, None] == ids[None, None, :], axis=1)
    flags = flags.astype(jnp.int32).reshape(-1)
    group_tokens = sources * tok_rows
    last = (jnp.arange(tiles, dtype=jnp.int32) * PARTS + part + 1) * tile_rows
    low = jnp.clip(tile_start[:, 0] - base_token, 0, group_tokens) // tok_rows
    high = (jnp.clip(last - base_token, 0, group_tokens) + tok_rows - 1) // tok_rows
    run = functools.partial(
        attention_kernel,
        part=part,
        prefixes=prefixes,
        local_pages=local_pages,
        tok_rows=tok_rows,
        q_scale=q_scale,
    )
    kv_rows = kv_group.reshape(-1, HEAD_SIZE)
    scores = 2 * tiles * tile_rows * kv_rows.shape[0] // 4
    return pl.pallas_call(
        run,
        out_shape=(
            jax.ShapeDtypeStruct((tiles, tile_rows, width), jnp.bfloat16),
            jax.ShapeDtypeStruct((tiles, 8, 2 * tile_rows), jnp.float32),
        ),
        grid_spec=pltpu.PrefetchScalarGridSpec(
            num_scalar_prefetch=6,
            grid=(tiles,),
            in_specs=[
                pl.BlockSpec((1, tile_rows, width), lambda i, *_: (i, 0, 0)),
                pl.BlockSpec((tile_rows, 1), lambda i, *_: (i, 0)),
                pl.BlockSpec((tile_rows, 1), lambda i, *_: (i, 0)),
                pl.BlockSpec(kv_rows.shape, lambda i, *_: (0, 0)),
            ],
            out_specs=[
                pl.BlockSpec((1, tile_rows, width), lambda i, *_: (i, 0, 0)),
                pl.BlockSpec((1, 8, 2 * tile_rows), lambda i, *_: (i, 0, 0)),
            ],
            scratch_shapes=[
                pltpu.VMEM((2 * tile_rows, HEAD_SIZE), jnp.float32),
                pltpu.VMEM((2 * tile_rows, HEAD_SIZE), jnp.float32),
            ],
        ),
        compiler_params=pltpu.CompilerParams(vmem_limit_bytes=32 * 1024 * 1024),
        cost_estimate=pl.CostEstimate(
            flops=16 * scores * HEAD_SIZE, bytes_accessed=8 * 1024 * 1024, transcendentals=2 * scores
        ),
        name="head_attention",
    )(places, offsets, flags, low, high, base_token[None], q_part,
      tile_start.reshape(-1, 1), tile_prefix.reshape(-1, 1), kv_rows)


def page_plan(owned, local_pages, tok_rows, prefixes):
    pages = owned.shape[0]
    place = jnp.arange(pages, dtype=jnp.int32)
    rank = owned * pages + place
    position = jnp.sum((rank[None, :] < rank[:, None]).astype(jnp.int32), axis=1)
    section = local_pages * PAGE_TOKENS + tok_rows
    row = place // local_pages * 2 * section + place % local_pages * PAGE_TOKENS
    places = jnp.sum((position[None, :] == place[:, None]).astype(jnp.int32) * row[None, :], axis=1)
    ids = jnp.arange(prefixes + 1, dtype=jnp.int32)
    offsets = jnp.sum((owned[None, :] < ids[:, None]).astype(jnp.int32), axis=1)
    return places, offsets


def two_halves(values):
    coarse = lax.reduce_precision(values, 8, 7)
    return [coarse.astype(jnp.bfloat16), (values - coarse).astype(jnp.bfloat16)]


def spread(block, axis="blk"):
    return lax.all_to_all(block, axis, 0, 0, tiled=True)


def finish(attention, residual, out_weight, post_gain):
    shares = lax.axis_size("kv")
    rows = attention.shape[0]
    projected = jnp.dot(attention, out_weight, preferred_element_type=jnp.float32)
    projected = projected.astype(jnp.bfloat16).reshape(rows, shares, -1).transpose(1, 0, 2)
    mine = jnp.sum(spread(projected, "kv").astype(jnp.float32), axis=0)
    mean_square = lax.psum(jnp.sum(mine * mine, axis=1), "kv") / D
    normed = mine * lax.rsqrt(mean_square + norm_eps)[:, None] * post_gain[None, :]
    return (residual.astype(jnp.float32) + normed).astype(jnp.bfloat16)


def body(
    suffix_query,
    suffix_key_value,
    suffix_resid,
    decode_query_rows,
    decode_key_value,
    decode_resid,
    out_weight,
    post_gain,
    prefix_page_store,
    prefix_table,
    decode_page_store,
    page_table,
    suffix_lengths,
    suffix_prefix,
    decode_ages,
):
    head_dim = HEAD_SIZE
    page_len = PAGE_TOKENS
    q_scale = (D // QUERY_HEADS) ** (-0.5)
    tok_rows = suffix_query.shape[0]
    q_heads = suffix_query.shape[1] // head_dim
    kv_heads = suffix_key_value.shape[2] // head_dim
    query_group_width = q_heads // kv_heads
    my_index = lax.axis_index("blk")
    blocks = lax.axis_size("blk")
    groups = blocks // kv_heads
    group = my_index // kv_heads
    pair = query_group_width * head_dim
    all_tokens = blocks * tok_rows
    part_rows = tok_rows // PARTS
    all_ids = jnp.arange(all_tokens, dtype=jnp.int32)
    tok_start, tok_prefix = token_tables(suffix_lengths, suffix_prefix, all_ids)
    pool_pages = prefix_table.shape[0]
    per_prefix = PREFIX_LENGTH // PAGE_TOKENS
    prefixes = pool_pages // per_prefix
    page_owner = (
        inverse_rows(prefix_table, jnp.arange(pool_pages, dtype=jnp.int32)) // per_prefix
    )
    local_pages = prefix_page_store.shape[1]
    group_pages = kv_heads * local_pages
    plan = page_plan(
        lax.dynamic_slice_in_dim(page_owner, group * group_pages, group_pages, 0),
        local_pages,
        tok_rows,
        prefixes,
    )
    q_heads_first = suffix_query.reshape(PARTS, part_rows, kv_heads, pair).transpose(0, 2, 1, 3)
    q_send = jnp.broadcast_to(
        q_heads_first[:, None], (PARTS, groups, kv_heads, part_rows, pair)
    ).reshape(PARTS, blocks, part_rows, pair)
    slot_rows = decode_query_rows.shape[0]
    decode_send = jnp.concatenate(
        [decode_query_rows, decode_key_value[0], decode_key_value[1]], axis=1
    )
    decode_width = decode_send.shape[1]
    decode_send = jnp.broadcast_to(
        decode_send.reshape(1, -1, pair), (blocks, slot_rows * decode_width // pair, pair)
    )
    first = spread(jnp.concatenate([q_send[0], decode_send], axis=1))
    kv_send = jnp.concatenate(
        [prefix_page_store.reshape(2, local_pages * page_len, -1), suffix_key_value], axis=1
    )
    kv_send = kv_send.reshape(2, -1, kv_heads, head_dim).transpose(2, 0, 1, 3)
    members = [[g * kv_heads + h for h in range(kv_heads)] for g in range(groups)]
    kv_group = lax.all_to_all(
        kv_send, "blk", 0, 0, tiled=True, axis_index_groups=members
    )
    q_parts = [first[:, :part_rows], spread(q_send[1])]
    decode_all = first[:, part_rows:].reshape(blocks * slot_rows, decode_width)
    all_dq = decode_all[:, : q_heads * head_dim]
    all_dkv = decode_all[:, q_heads * head_dim :].reshape(-1, 2, kv_heads * head_dim)
    all_dkv = all_dkv.transpose(1, 0, 2)
    slot_total = all_dq.shape[0]
    slot_pages = SLOT_CAPACITY // PAGE_TOKENS
    local_cache = decode_page_store.shape[1]
    page_ids = my_index * local_cache + jnp.arange(local_cache, dtype=jnp.int32)
    position = inverse_rows(page_table, page_ids)
    slot_of = position // slot_pages
    block_of = position % slot_pages
    slot_hot = slot_of[:, None] == jnp.arange(slot_total, dtype=jnp.int32)[None, :]
    page_age = jnp.sum(slot_hot.astype(jnp.int32) * decode_ages[None, :], axis=1)
    select = slot_hot.astype(jnp.bfloat16)
    new_rows = jnp.einsum(
        "ls,tsc->tlc", select, all_dkv, preferred_element_type=jnp.float32
    ).astype(jnp.bfloat16)
    write_here = (block_of == page_age // page_len)[:, None] & (
        jnp.arange(page_len, dtype=jnp.int32)[None, :] == (page_age % page_len)[:, None]
    )
    new_cache = jnp.where(write_here[None, :, :, None], new_rows[:, :, None, :], decode_page_store)
    page_queries = jnp.dot(select, all_dq, preferred_element_type=jnp.float32).astype(jnp.bfloat16)
    page_queries = page_queries.reshape(local_cache, kv_heads, query_group_width, head_dim)
    key_cache = new_cache[0].reshape(local_cache, page_len, kv_heads, head_dim)
    value_cache = new_cache[1].reshape(local_cache, page_len, kv_heads, head_dim)
    logits = (
        jnp.einsum("lhgd,lphd->lhgp", page_queries, key_cache, preferred_element_type=jnp.float32)
        * q_scale
    )
    capped = soft_cap * jnp.tanh(logits / soft_cap)
    places = block_of[:, None] * page_len + jnp.arange(page_len, dtype=jnp.int32)[None, :]
    seen_pos = places <= page_age[:, None]
    weights = jnp.where(seen_pos[:, None, None, :], jnp.exp(capped), 0.0)
    page_denom = jnp.sum(weights, axis=3)
    page_numer = jnp.einsum(
        "lhgp,lphd->lhgd",
        weights.astype(jnp.bfloat16),
        value_cache,
        preferred_element_type=jnp.float32,
    )
    slot_float = slot_hot.astype(jnp.float32)
    slot_numer = jnp.einsum(
        "ls,lhgd->shgd", slot_float, page_numer, precision=lax.Precision.HIGHEST
    )
    slot_denom = jnp.einsum("ls,lhg->shg", slot_float, page_denom, precision=lax.Precision.HIGHEST)
    slot_numer = slot_numer.astype(jnp.bfloat16).reshape(blocks, -1, pair)
    slot_denom = slot_denom.reshape(blocks, -1)
    decode_rows_sent = slot_numer.shape[1]
    decode_sums = slot_denom.shape[1]
    half_sums = query_group_width * part_rows
    hidden = []
    for part in range(PARTS):
        numer, denom = head_attention(
            part,
            q_parts[part],
            kv_group,
            tok_start,
            tok_prefix,
            plan,
            group * kv_heads * tok_rows,
            prefixes,
            local_pages,
            tok_rows,
            q_scale,
        )
        sums = two_halves(denom[:, 0, :])
        blocks_sent = [numer]
        if part == 0:
            sums = sums + two_halves(slot_denom)
            blocks_sent.append(slot_numer)
        sums = jnp.concatenate(sums, axis=1)
        sums = jnp.pad(sums, ((0, 0), (0, -sums.shape[1] % pair))).reshape(blocks, -1, pair)
        got = spread(jnp.concatenate(blocks_sent + [sums], axis=1))
        numer = got[:, :part_rows].reshape(
            groups, kv_heads, part_rows, query_group_width, head_dim
        )
        numer = jnp.sum(numer.astype(jnp.float32), axis=0)
        sums = got[:, -sums.shape[1] :].reshape(blocks, -1).astype(jnp.float32)
        denom = sums[:, :half_sums] + sums[:, half_sums : 2 * half_sums]
        denom = jnp.sum(
            denom.reshape(groups, kv_heads, query_group_width, part_rows), axis=0
        )
        attention = numer / denom.transpose(0, 2, 1)[..., None]
        attention = attention.astype(jnp.bfloat16).transpose(1, 0, 2, 3)
        attention = attention.reshape(part_rows, q_heads * head_dim)
        residual = suffix_resid[part * part_rows : (part + 1) * part_rows]
        if part == 0:
            mine_numer = got[:, part_rows : part_rows + decode_rows_sent].astype(jnp.float32)
            mine_numer = jnp.sum(mine_numer, axis=0).reshape(slot_rows, q_heads, head_dim)
            mine_denom = sums[:, 2 * half_sums : 2 * half_sums + 2 * decode_sums]
            mine_denom = jnp.sum(mine_denom.reshape(2 * blocks, slot_rows, q_heads), axis=0)
            decode_attn = (mine_numer / mine_denom[..., None]).astype(jnp.bfloat16)
            decode_attn = decode_attn.reshape(slot_rows, q_heads * head_dim)
            attention = jnp.concatenate([attention, decode_attn], axis=0)
            residual = jnp.concatenate([residual, decode_resid], axis=0)
        hidden.append(finish(attention, residual, out_weight, post_gain))
    suffix_hidden = jnp.concatenate([hidden[0][:part_rows], hidden[1]], axis=0)
    return (suffix_hidden, hidden[0][part_rows:], new_cache)


def solution(mesh):
    placed = (
        P("blk", "kv"),
        P(None, "blk", "kv"),
        P("blk", "kv"),
        P("blk", "kv"),
        P(None, "blk", "kv"),
        P("blk", "kv"),
        P("kv", None),
        P("kv"),
        P(None, "blk", None, "kv"),
        P(),
        P(None, "blk", None, "kv"),
        P(),
        P(),
        P(),
        P(),
    )
    return jax.shard_map(
        body,
        mesh=mesh,
        in_specs=placed,
        out_specs=(P("blk", "kv"), P("blk", "kv"), P(None, "blk", None, "kv")),
        check_vma=False,
    )
```

```python
import functools
import math

import jax
import jax.numpy as jnp
from jax import lax
from jax.experimental import pallas as pl
from jax.experimental.pallas import tpu as pltpu
from jax.sharding import PartitionSpec as P

D = 4608
QUERY_HEADS = 32
HEAD_SIZE = 128
PAGE_TOKENS = 128
PREFIX_LENGTH = 3072
SLOT_CAPACITY = 1024


soft_cap = 50.0
norm_eps = 1e-06


def token_tables(lengths, prefix_ids, token_ids):
    suffix_ends = jnp.cumsum(lengths)
    starts = suffix_ends - lengths
    inside = (
        (token_ids[:, None] >= starts[None, :]) & (token_ids[:, None] < suffix_ends[None, :])
    ).astype(jnp.int32)
    tok_start = jnp.sum(inside * starts[None, :], axis=1)
    tok_prefix = jnp.sum(inside * prefix_ids[None, :], axis=1)
    return (tok_start, tok_prefix)


def inverse_rows(table, wanted):
    hits = (table[None, :] == wanted[:, None]).astype(jnp.int32)
    places = jnp.arange(table.shape[0], dtype=jnp.int32)
    return jnp.sum(hits * places[None, :], axis=1)


PARTS = 2
STRIDE = 4


def attention_kernel(
    places,
    offsets,
    flags,
    low,
    high,
    group_base,
    q_ref,
    start_ref,
    prefix_ref,
    kv_ref,
    numer_ref,
    denom_ref,
    acc,
    wacc,
    *,
    part,
    prefixes,
    local_pages,
    tok_rows,
    sources,
    q_scale,
):
    page_len = PAGE_TOKENS
    tile_rows = q_ref.shape[1]
    section = local_pages * page_len + tok_rows
    tile = pl.program_id(0)
    tokens = pl.num_programs(0) * PARTS * tile_rows
    q = q_ref[0]
    half = HEAD_SIZE
    rows_q = jnp.concatenate([q[:, :half], q[:, half:]], axis=0)
    row_prefix = prefix_ref[...]
    row_prefix = jnp.concatenate([row_prefix, row_prefix], axis=0)
    row_start = start_ref[...]
    row_start = jnp.concatenate([row_start, row_start], axis=0)
    inner = q_scale / soft_cap
    outer = soft_cap * math.log2(math.e)

    def weights_of(key_rows):
        logits = lax.dot_general(
            rows_q, key_rows, (((1,), (1,)), ((), ())), preferred_element_type=jnp.float32
        )
        return jnp.exp2(jnp.tanh(logits * inner) * outer)

    def folded(w):
        out = w[:, :half]
        for k in range(1, w.shape[1] // half):
            out = out + w[:, k * half : (k + 1) * half]
        return out

    def load(row, length):
        return kv_ref[pl.ds(pl.multiple_of(row, 64), length), :]

    row_id = (tile * PARTS + part) * tile_rows + lax.broadcasted_iota(
        jnp.int32, (tile_rows, 1), 0
    )
    row_id = jnp.concatenate([row_id, row_id], axis=0)
    acc[...] = jnp.zeros_like(acc)
    wacc[...] = jnp.zeros_like(wacc)
    span = 256

    def own(c, carry):
        key_rows, value_rows, seen = [], [], []
        for k in range(2):
            source = low[tile] + 2 * c + k
            first = group_base[0] + source * tok_rows
            row = (2 * jnp.minimum(source, sources - 1) + 1) * section - span
            key_id = first + (tok_rows - span) + lax.broadcasted_iota(jnp.int32, (1, span), 1)
            within = jnp.where(source < high[tile], first, tokens)
            seen.append((key_id >= jnp.maximum(row_start, within)) & (key_id <= row_id))
            key_rows.append(load(row, span))
            value_rows.append(load(row + section, span))
        w = weights_of(jnp.concatenate(key_rows, axis=0))
        w = jnp.concatenate(
            [jnp.where(seen[k], w[:, k * span : (k + 1) * span], 0.0) for k in range(2)], axis=1
        )
        acc[...] += jnp.dot(
            w.astype(jnp.bfloat16),
            jnp.concatenate(value_rows, axis=0),
            preferred_element_type=jnp.float32,
        )
        wacc[...] += folded(w)
        return carry

    lax.fori_loop(0, (jnp.maximum(high[tile] - low[tile], 0) + 1) // 2, own, 0)

    def step(keep, first, width, count):
        rows = [places[first + jnp.minimum(k, count - 1)] for k in range(width)]
        key_rows = jnp.concatenate([load(r, page_len) for r in rows], axis=0)
        value_rows = jnp.concatenate([load(r + section, page_len) for r in rows], axis=0)
        w = weights_of(key_rows)
        sure = (width - STRIDE) * page_len
        column = lax.broadcasted_iota(jnp.int32, (1, STRIDE * page_len), 1) + sure
        ending = jnp.where(column < count * page_len, w[:, sure:], 0.0)
        w = jnp.concatenate([w[:, :sure], ending], axis=1) if sure else ending
        num = jnp.dot(w.astype(jnp.bfloat16), value_rows, preferred_element_type=jnp.float32)
        acc[...] += num * keep
        wacc[...] += folded(w) * keep

    def one_prefix(p, carry):
        begin = offsets[p]
        count = jnp.where(flags[tile * prefixes + p] != 0, offsets[p + 1] - begin, 0)
        keep = jnp.where(row_prefix == p, 1.0, 0.0)
        longest = 4 * STRIDE
        loops = jnp.maximum(count - 1, 0) // longest

        def full(c, inner_carry):
            step(keep, begin + c * longest, longest, longest)
            return inner_carry

        lax.fori_loop(0, loops, full, 0)
        rest = count - loops * longest
        for width in range(STRIDE, longest + 1, STRIDE):

            @pl.when((rest > width - STRIDE) & (rest <= width))
            def _():
                step(keep, begin + loops * longest, width, rest)

        return carry

    lax.fori_loop(0, prefixes, one_prefix, 0)

    numer_ref[0] = jnp.concatenate(
        [acc[:tile_rows, :], acc[tile_rows:, :]], axis=1
    ).astype(numer_ref.dtype)
    denom_ref[0] = lax.dot_general(
        jnp.ones((8, half), jnp.float32),
        wacc[...],
        (((1,), (1,)), ((), ())),
        preferred_element_type=jnp.float32,
        precision=lax.Precision.HIGHEST,
    )


def head_attention(part, q_part, kv_group, tok_start, tok_prefix, plan, base_token,
                   prefixes, local_pages, tok_rows, q_scale):
    tiles, tile_rows, width = q_part.shape
    sources = kv_group.shape[0]
    places, offsets = plan
    tile_start = tok_start.reshape(tiles, PARTS, tile_rows)[:, part]
    tile_prefix = tok_prefix.reshape(tiles, PARTS, tile_rows)[:, part]
    ids = jnp.arange(prefixes, dtype=jnp.int32)
    flags = jnp.any(tile_prefix[:, :, None] == ids[None, None, :], axis=1)
    flags = flags.astype(jnp.int32).reshape(-1)
    group_tokens = sources * tok_rows
    last = (jnp.arange(tiles, dtype=jnp.int32) * PARTS + part + 1) * tile_rows
    low = jnp.clip(tile_start[:, 0] - base_token, 0, group_tokens) // tok_rows
    high = (jnp.clip(last - base_token, 0, group_tokens) + tok_rows - 1) // tok_rows
    run = functools.partial(
        attention_kernel,
        part=part,
        prefixes=prefixes,
        local_pages=local_pages,
        tok_rows=tok_rows,
        sources=sources,
        q_scale=q_scale,
    )
    kv_rows = kv_group.reshape(-1, HEAD_SIZE)
    scores = 2 * tiles * tile_rows * kv_rows.shape[0] // 4
    return pl.pallas_call(
        run,
        out_shape=(
            jax.ShapeDtypeStruct((tiles, tile_rows, width), jnp.bfloat16),
            jax.ShapeDtypeStruct((tiles, 8, 2 * tile_rows), jnp.float32),
        ),
        grid_spec=pltpu.PrefetchScalarGridSpec(
            num_scalar_prefetch=6,
            grid=(tiles,),
            in_specs=[
                pl.BlockSpec((1, tile_rows, width), lambda i, *_: (i, 0, 0)),
                pl.BlockSpec((tile_rows, 1), lambda i, *_: (i, 0)),
                pl.BlockSpec((tile_rows, 1), lambda i, *_: (i, 0)),
                pl.BlockSpec(kv_rows.shape, lambda i, *_: (0, 0)),
            ],
            out_specs=[
                pl.BlockSpec((1, tile_rows, width), lambda i, *_: (i, 0, 0)),
                pl.BlockSpec((1, 8, 2 * tile_rows), lambda i, *_: (i, 0, 0)),
            ],
            scratch_shapes=[
                pltpu.VMEM((2 * tile_rows, HEAD_SIZE), jnp.float32),
                pltpu.VMEM((2 * tile_rows, HEAD_SIZE), jnp.float32),
            ],
        ),
        compiler_params=pltpu.CompilerParams(vmem_limit_bytes=32 * 1024 * 1024),
        cost_estimate=pl.CostEstimate(
            flops=16 * scores * HEAD_SIZE, bytes_accessed=8 * 1024 * 1024, transcendentals=2 * scores
        ),
        name="head_attention",
    )(places, offsets, flags, low, high, base_token[None], q_part,
      tile_start.reshape(-1, 1), tile_prefix.reshape(-1, 1), kv_rows)


def page_plan(owned, local_pages, tok_rows, prefixes):
    pages = owned.shape[0]
    place = jnp.arange(pages, dtype=jnp.int32)
    rank = owned * pages + place
    position = jnp.sum((rank[None, :] < rank[:, None]).astype(jnp.int32), axis=1)
    section = local_pages * PAGE_TOKENS + tok_rows
    row = place // local_pages * 2 * section + place % local_pages * PAGE_TOKENS
    places = jnp.sum((position[None, :] == place[:, None]).astype(jnp.int32) * row[None, :], axis=1)
    ids = jnp.arange(prefixes + 1, dtype=jnp.int32)
    offsets = jnp.sum((owned[None, :] < ids[:, None]).astype(jnp.int32), axis=1)
    return places, offsets


def two_halves(values):
    coarse = lax.reduce_precision(values, 8, 7)
    return [coarse.astype(jnp.bfloat16), (values - coarse).astype(jnp.bfloat16)]


def spread(block, axis="blk"):
    return lax.all_to_all(block, axis, 0, 0, tiled=True)


def finish(attention, residual, out_weight, post_gain):
    shares = lax.axis_size("kv")
    rows = attention.shape[0]
    projected = jnp.dot(attention, out_weight, preferred_element_type=jnp.float32)
    projected = projected.astype(jnp.bfloat16).reshape(rows, shares, -1).transpose(1, 0, 2)
    mine = jnp.sum(spread(projected, "kv").astype(jnp.float32), axis=0)
    mean_square = lax.psum(jnp.sum(mine * mine, axis=1), "kv") / D
    normed = mine * lax.rsqrt(mean_square + norm_eps)[:, None] * post_gain[None, :]
    return (residual.astype(jnp.float32) + normed).astype(jnp.bfloat16)


def body(
    suffix_query,
    suffix_key_value,
    suffix_resid,
    decode_query_rows,
    decode_key_value,
    decode_resid,
    out_weight,
    post_gain,
    prefix_page_store,
    prefix_table,
    decode_page_store,
    page_table,
    suffix_lengths,
    suffix_prefix,
    decode_ages,
):
    head_dim = HEAD_SIZE
    page_len = PAGE_TOKENS
    q_scale = (D // QUERY_HEADS) ** (-0.5)
    tok_rows = suffix_query.shape[0]
    q_heads = suffix_query.shape[1] // head_dim
    kv_heads = suffix_key_value.shape[2] // head_dim
    query_group_width = q_heads // kv_heads
    my_index = lax.axis_index("blk")
    blocks = lax.axis_size("blk")
    groups = blocks // kv_heads
    group = my_index // kv_heads
    pair = query_group_width * head_dim
    all_tokens = blocks * tok_rows
    part_rows = tok_rows // PARTS
    all_ids = jnp.arange(all_tokens, dtype=jnp.int32)
    tok_start, tok_prefix = token_tables(suffix_lengths, suffix_prefix, all_ids)
    pool_pages = prefix_table.shape[0]
    per_prefix = PREFIX_LENGTH // PAGE_TOKENS
    prefixes = pool_pages // per_prefix
    page_owner = (
        inverse_rows(prefix_table, jnp.arange(pool_pages, dtype=jnp.int32)) // per_prefix
    )
    local_pages = prefix_page_store.shape[1]
    group_pages = kv_heads * local_pages
    plan = page_plan(
        lax.dynamic_slice_in_dim(page_owner, group * group_pages, group_pages, 0),
        local_pages,
        tok_rows,
        prefixes,
    )
    q_heads_first = suffix_query.reshape(PARTS, part_rows, kv_heads, pair).transpose(0, 2, 1, 3)
    q_send = jnp.broadcast_to(
        q_heads_first[:, None], (PARTS, groups, kv_heads, part_rows, pair)
    ).reshape(PARTS, blocks, part_rows, pair)
    slot_rows = decode_query_rows.shape[0]
    decode_send = jnp.concatenate(
        [decode_query_rows, decode_key_value[0], decode_key_value[1]], axis=1
    )
    decode_width = decode_send.shape[1]
    decode_send = jnp.broadcast_to(
        decode_send.reshape(1, -1, pair), (blocks, slot_rows * decode_width // pair, pair)
    )
    first = spread(jnp.concatenate([q_send[0], decode_send], axis=1))
    kv_send = jnp.concatenate(
        [prefix_page_store.reshape(2, local_pages * page_len, -1), suffix_key_value], axis=1
    )
    kv_send = kv_send.reshape(2, -1, kv_heads, head_dim).transpose(2, 0, 1, 3)
    first, kv_send = lax.optimization_barrier((first, kv_send))
    members = [[g * kv_heads + h for h in range(kv_heads)] for g in range(groups)]
    kv_group = lax.all_to_all(
        kv_send, "blk", 0, 0, tiled=True, axis_index_groups=members
    )
    decode_all = first[:, part_rows:].reshape(blocks * slot_rows, decode_width)
    all_dq = decode_all[:, : q_heads * head_dim]
    all_dkv = decode_all[:, q_heads * head_dim :].reshape(-1, 2, kv_heads * head_dim)
    all_dkv = all_dkv.transpose(1, 0, 2)
    slot_total = all_dq.shape[0]
    slot_pages = SLOT_CAPACITY // PAGE_TOKENS
    local_cache = decode_page_store.shape[1]
    page_ids = my_index * local_cache + jnp.arange(local_cache, dtype=jnp.int32)
    position = inverse_rows(page_table, page_ids)
    slot_of = position // slot_pages
    block_of = position % slot_pages
    slot_hot = slot_of[:, None] == jnp.arange(slot_total, dtype=jnp.int32)[None, :]
    page_age = jnp.sum(slot_hot.astype(jnp.int32) * decode_ages[None, :], axis=1)
    select = slot_hot.astype(jnp.bfloat16)
    new_rows = jnp.einsum(
        "ls,tsc->tlc", select, all_dkv, preferred_element_type=jnp.float32
    ).astype(jnp.bfloat16)
    write_here = (block_of == page_age // page_len)[:, None] & (
        jnp.arange(page_len, dtype=jnp.int32)[None, :] == (page_age % page_len)[:, None]
    )
    new_cache = jnp.where(write_here[None, :, :, None], new_rows[:, :, None, :], decode_page_store)
    page_queries = jnp.dot(select, all_dq, preferred_element_type=jnp.float32).astype(jnp.bfloat16)
    page_queries = page_queries.reshape(local_cache, kv_heads, query_group_width, head_dim)
    key_cache = new_cache[0].reshape(local_cache, page_len, kv_heads, head_dim)
    value_cache = new_cache[1].reshape(local_cache, page_len, kv_heads, head_dim)
    logits = (
        jnp.einsum("lhgd,lphd->lhgp", page_queries, key_cache, preferred_element_type=jnp.float32)
        * q_scale
    )
    capped = soft_cap * jnp.tanh(logits / soft_cap)
    places = block_of[:, None] * page_len + jnp.arange(page_len, dtype=jnp.int32)[None, :]
    seen_pos = places <= page_age[:, None]
    weights = jnp.where(seen_pos[:, None, None, :], jnp.exp(capped), 0.0)
    page_denom = jnp.sum(weights, axis=3)
    page_numer = jnp.einsum(
        "lhgp,lphd->lhgd",
        weights.astype(jnp.bfloat16),
        value_cache,
        preferred_element_type=jnp.float32,
    )
    slot_float = slot_hot.astype(jnp.float32)
    slot_numer = jnp.einsum(
        "ls,lhgd->shgd", slot_float, page_numer, precision=lax.Precision.HIGHEST
    )
    slot_denom = jnp.einsum("ls,lhg->shg", slot_float, page_denom, precision=lax.Precision.HIGHEST)
    slot_numer = slot_numer.astype(jnp.bfloat16).reshape(blocks, -1, pair)
    slot_denom = slot_denom.reshape(blocks, -1)
    q_late, kv_group, slot_numer, slot_denom = lax.optimization_barrier(
        (q_send[1], kv_group, slot_numer, slot_denom)
    )
    q_parts = [first[:, :part_rows], spread(q_late)]
    decode_rows_sent = slot_numer.shape[1]
    decode_sums = slot_denom.shape[1]
    half_sums = query_group_width * part_rows
    hidden = []
    for part in range(PARTS):
        numer, denom = head_attention(
            part,
            q_parts[part],
            kv_group,
            tok_start,
            tok_prefix,
            plan,
            group * kv_heads * tok_rows,
            prefixes,
            local_pages,
            tok_rows,
            q_scale,
        )
        sums = two_halves(denom[:, 0, :])
        blocks_sent = [numer]
        if part == 0:
            sums = sums + two_halves(slot_denom)
            blocks_sent.append(slot_numer)
        sums = jnp.concatenate(sums, axis=1)
        sums = jnp.pad(sums, ((0, 0), (0, -sums.shape[1] % pair))).reshape(blocks, -1, pair)
        got = spread(jnp.concatenate(blocks_sent + [sums], axis=1))
        numer = got[:, :part_rows].reshape(
            groups, kv_heads, part_rows, query_group_width, head_dim
        )
        numer = jnp.sum(numer.astype(jnp.float32), axis=0)
        sums = got[:, -sums.shape[1] :].reshape(blocks, -1).astype(jnp.float32)
        denom = sums[:, :half_sums] + sums[:, half_sums : 2 * half_sums]
        denom = jnp.sum(
            denom.reshape(groups, kv_heads, query_group_width, part_rows), axis=0
        )
        attention = numer / denom.transpose(0, 2, 1)[..., None]
        attention = attention.astype(jnp.bfloat16).transpose(1, 0, 2, 3)
        attention = attention.reshape(part_rows, q_heads * head_dim)
        residual = suffix_resid[part * part_rows : (part + 1) * part_rows]
        if part == 0:
            mine_numer = got[:, part_rows : part_rows + decode_rows_sent].astype(jnp.float32)
            mine_numer = jnp.sum(mine_numer, axis=0).reshape(slot_rows, q_heads, head_dim)
            mine_denom = sums[:, 2 * half_sums : 2 * half_sums + 2 * decode_sums]
            mine_denom = jnp.sum(mine_denom.reshape(2 * blocks, slot_rows, q_heads), axis=0)
            decode_attn = (mine_numer / mine_denom[..., None]).astype(jnp.bfloat16)
            decode_attn = decode_attn.reshape(slot_rows, q_heads * head_dim)
            attention = jnp.concatenate([attention, decode_attn], axis=0)
            residual = jnp.concatenate([residual, decode_resid], axis=0)
        hidden.append(finish(attention, residual, out_weight, post_gain))
    suffix_hidden = jnp.concatenate([hidden[0][:part_rows], hidden[1]], axis=0)
    return (suffix_hidden, hidden[0][part_rows:], new_cache)


def solution(mesh):
    placed = (
        P("blk", "kv"),
        P(None, "blk", "kv"),
        P("blk", "kv"),
        P("blk", "kv"),
        P(None, "blk", "kv"),
        P("blk", "kv"),
        P("kv", None),
        P("kv"),
        P(None, "blk", None, "kv"),
        P(),
        P(None, "blk", None, "kv"),
        P(),
        P(),
        P(),
        P(),
    )
    return jax.shard_map(
        body,
        mesh=mesh,
        in_specs=placed,
        out_specs=(P("blk", "kv"), P("blk", "kv"), P(None, "blk", None, "kv")),
        check_vma=False,
    )
```
